512 devices in a mesh: head: 16 (over y_lo, z), blk: 32 (over y_hi, x, core).
Axes of the slice: x: 4, y: 8 (y_hi: 4, y_lo: 2; y = y_hi * 2 + y_lo), z: 8, core: 2. Of those that a mesh axis runs over, the one named last changes fastest.
Arguments:
- query_rows: bfloat16 [65536, 1024], P(('blk', 'head')), may hold values from -300 to 300
- key_rows: bfloat16 [65536, 1024], P(('blk', 'head')), may hold values from -4 to 4
- value_rows: bfloat16 [65536, 1024], P(('blk', 'head')), may hold values from -6 to 6
- out_grad: bfloat16 [65536, 1024], P(('blk', 'head')), may hold values from -96 to 96
- block_pairs: int32 [512, 8], replicated, may hold values from 0 to 511, as said below
Outputs:
- grad_query: bfloat16 [65536, 1024], P(('blk', 'head'))
- grad_key: bfloat16 [65536, 1024], P(('blk', 'head'))
- grad_value: bfloat16 [65536, 1024], P(('blk', 'head'))
The draws below stay inside these ranges and needn't reach their ends.
Inputs may be any that keep to these rules, and one draw needn't show every extreme that they name: `block_pairs`: row b names 8 different blocks: b itself first, the others among the blocks of the shard of 2048 tokens that holds b and of the shards just before and after it, counted around a closed loop of all shards.
All inputs are finite; a program needn't handle non-finite values.
Results may differ from the reference program's by a relative error of at most 0.007.
Values may be sent and summed in bfloat16 or wider, within the bound.
A program may use at most 64 MiB of HBM per device.

```python
import math
import jax
import jax.numpy as jnp
from jax import lax

HEADS = 16
HEAD_DIM = 64
QB = 128
NNB = 8
TOKENS = 65536
SHARD = 2048
NB = 512


def shared_parts(key):
    base_rows = jnp.clip(jax.random.normal(jax.random.fold_in(key, 11), (TOKENS, HEADS * HEAD_DIM), jnp.float32), -4.0, 4.0)
    return base_rows


def draw_key_rows(key, part):
    base_rows = shared_parts(key)
    result = base_rows
    return result.astype(jnp.bfloat16)


def draw_query_rows(key, part):
    key = jax.random.fold_in(key, 5)
    fresh_rows = jnp.clip(jax.random.normal(key, (TOKENS, HEADS * HEAD_DIM), jnp.float32), -6.0, 6.0)
    result = fresh_rows
    return result.astype(jnp.bfloat16)


def draw_block_pairs(key, part):
    key = jax.random.fold_in(key, 7)
    per_shard = SHARD // QB
    row_keys = jax.random.split(key, NB)
    others = jax.vmap(lambda one_key: jax.random.permutation(one_key, 3 * per_shard - 1))(row_keys)[:, :NNB - 1]
    block_index = jnp.arange(NB, dtype=jnp.int32)
    own_offset = per_shard + block_index % per_shard
    offsets = jnp.where(others >= own_offset[:, None], others + 1, others)
    window_start = (block_index // per_shard - 1) * per_shard
    picked = (window_start[:, None] + offsets) % NB
    return jnp.concatenate([block_index[:, None], picked], 1).astype(jnp.int32)


def block_levels(stream_key, shape, cuts, smallest, high):
    gain = 1.0
    for dim, parts in cuts:
        steps = jax.random.uniform(jax.random.fold_in(jax.random.fold_in(stream_key, 6), dim), (parts,), jnp.float32, smallest / len(cuts), high / len(cuts))
        gain = gain * jnp.repeat(jnp.exp(steps), shape[dim] // parts).reshape((-1,) + (1,) * (len(shape) - 1 - dim))
    return gain


def bell_draw(own_key, extent, spread, bound, cuts=(), kind=jnp.bfloat16):
    values = spread * jax.random.normal(own_key, extent, jnp.float32)
    if cuts:
        values = values * block_levels(own_key, extent, cuts, -0.22, 0.18)
    return jnp.clip(values, -bound, bound).astype(kind)


def setup_inputs(seed: int = 0) -> dict:
    splits = jax.random.split(jax.random.key(seed), 6)
    return {
        "query_rows": draw_query_rows(jax.random.fold_in(splits[5], 71), 0),
        "key_rows": draw_key_rows(jax.random.fold_in(splits[5], 71), 0),
        "value_rows": bell_draw(splits[2], (TOKENS, HEADS * HEAD_DIM), 1.0, 6.0, ((0, 512),)),
        "out_grad": bell_draw(splits[3], (TOKENS, HEADS * HEAD_DIM), 16.0, 96.0, ((0, 512),)),
        "block_pairs": draw_block_pairs(jax.random.fold_in(splits[5], 71), 0),
    }


def reference(query_rows, key_rows, value_rows, out_grad, block_pairs):
    score_scale = HEAD_DIM ** -0.5
    group_size = math.gcd(NB, max(1, 512 // QB))
    block_shape = (NB, QB, HEADS, HEAD_DIM)
    queries = query_rows.reshape(block_shape)
    keys_all = key_rows.reshape(block_shape)
    values_all = value_rows.reshape(block_shape)
    grads_all = out_grad.reshape(block_shape)

    def group_step(running, group_index):
        key_acc, value_acc = running
        first = group_index * group_size
        q_group = lax.dynamic_slice_in_dim(queries, first, group_size, 0).astype(jnp.float32)
        d_group = lax.dynamic_slice_in_dim(grads_all, first, group_size, 0).astype(jnp.float32)
        block_ids = lax.dynamic_slice_in_dim(block_pairs, first, group_size, 0).reshape(-1).astype(jnp.int32)
        gathered_keys = jnp.take(keys_all, block_ids, axis=0).astype(jnp.float32).reshape(group_size, NNB * QB, HEADS, HEAD_DIM)
        gathered_values = jnp.take(values_all, block_ids, axis=0).astype(jnp.float32).reshape(group_size, NNB * QB, HEADS, HEAD_DIM)
        scores = jnp.einsum("gqhd,gkhd->ghqk", q_group, gathered_keys) * score_scale
        row_top = jnp.max(scores, -1, keepdims=True)
        exp_scores = jnp.exp(scores - row_top)
        row_total = jnp.sum(exp_scores, -1, keepdims=True)
        soft_probs = exp_scores / row_total
        grad_probs = jnp.einsum("gqhd,gkhd->ghqk", d_group, gathered_values)
        row_delta = jnp.sum(soft_probs * grad_probs, -1, keepdims=True)
        score_grad = lax.optimization_barrier((soft_probs * (grad_probs - row_delta) * score_scale).astype(jnp.bfloat16)).astype(jnp.float32)
        probs_low = lax.optimization_barrier(soft_probs.astype(jnp.bfloat16)).astype(jnp.float32)
        grad_q = jnp.einsum("ghqk,gkhd->gqhd", score_grad, gathered_keys).astype(jnp.bfloat16)
        part_k = jnp.einsum("ghqk,gqhd->gkhd", score_grad, q_group).reshape(group_size * NNB, QB, HEADS, HEAD_DIM)
        part_v = jnp.einsum("ghqk,gqhd->gkhd", probs_low, d_group).reshape(group_size * NNB, QB, HEADS, HEAD_DIM)
        key_acc = key_acc.at[block_ids].add(part_k)
        value_acc = value_acc.at[block_ids].add(part_v)
        return (key_acc, value_acc), grad_q

    zeros_acc = jnp.zeros(block_shape, jnp.float32)
    steps_all = jnp.arange(NB // group_size, dtype=jnp.int32)
    (key_acc, value_acc), grad_q = lax.scan(group_step, (zeros_acc, zeros_acc), steps_all)
    flat_shape = (TOKENS, HEADS * HEAD_DIM)
    return (grad_q.reshape(flat_shape), key_acc.reshape(flat_shape).astype(jnp.bfloat16), value_acc.reshape(flat_shape).astype(jnp.bfloat16))
```

```python
import functools

import jax
import jax.numpy as jnp
from jax import lax
from jax.experimental import pallas as pl
from jax.experimental.pallas import tpu as pltpu
from jax.sharding import PartitionSpec as P

HD = 64
QB = 128
NNB = 8
MESH = pl.DeviceIdType.MESH
BF16 = jnp.bfloat16
F32 = jnp.float32


def kernel(
    n,
    meta,
    q_ref,
    k_ref,
    v_ref,
    d_ref,
    gq_ref,
    gk_ref,
    gv_ref,
    kv_send,
    qd_send,
    kv_win,
    kt_win,
    qd_all,
    st,
    w,
    parts,
    run,
    dq_send,
    dq_recv,
    part_send,
    part_recv,
    out_send,
    out_recv,
    kv_ss,
    kv_rs,
    fw_ss,
    fw_rs,
    qd_ss,
    qd_rs,
    dq_ss,
    dq_rs,
    pt_ss,
    pt_rs,
    ot_ss,
    ot_rs,
):
    blk, me = lax.axis_index("blk"), lax.axis_index("head")
    nblk = lax.axis_size("blk")
    before, after = lax.rem(blk + nblk - 1, nblk), lax.rem(blk + 1, nblk)
    pairs = n * NNB
    at_order, at_keep, at_last, at_has = pairs, 2 * pairs, 3 * pairs, 3 * pairs + 3 * n

    def peer(t):
        return lax.rem(me + t, n)

    def source(t):
        return lax.rem(me - t + n, n)

    def remote(src, dst, ss, rs, b, h):
        return pltpu.make_async_remote_copy(
            src_ref=src, dst_ref=dst, send_sem=ss, recv_sem=rs, device_id={"blk": b, "head": h}, device_id_type=MESH
        )

    def kv_copy(to):
        return remote(kv_send.at[to], kv_win.at[n + me], kv_ss.at[to], kv_rs.at[me], blk, to)

    def kv_arrival(src):
        return remote(kv_send.at[src], kv_win.at[n + src], kv_ss.at[src], kv_rs.at[src], blk, src)

    def qd_copy(to):
        return remote(qd_send.at[to], qd_all.at[me], qd_ss.at[to], qd_rs.at[me], blk, to)

    def qd_arrival(src):
        return remote(qd_send.at[src], qd_all.at[src], qd_ss.at[src], qd_rs.at[src], blk, src)

    def fw_copy(side, i):
        dst = kv_win.at[i] if side == 0 else kv_win.at[2 * n + i]
        return remote(
            kv_win.at[n + i], dst, fw_ss.at[side, i], fw_rs.at[side, i], after if side == 0 else before, me
        )

    def pt_copy(side, i):
        return remote(
            part_send.at[side, i],
            part_recv.at[side, i],
            pt_ss.at[side, i],
            pt_rs.at[side, i],
            before if side == 0 else after,
            me,
        )

    def dq_copy(to):
        rows = pl.ds(pl.multiple_of(me * HD, HD), HD)
        return remote(dq_send.at[to], dq_recv.at[rows], dq_ss.at[to], dq_rs.at[me], blk, to)

    def dq_arrival(src):
        rows = pl.ds(pl.multiple_of(src * HD, HD), HD)
        return remote(dq_send.at[src], dq_recv.at[rows], dq_ss.at[src], dq_rs.at[src], blk, src)

    def ot_copy(to):
        return remote(out_send.at[to], out_recv.at[me], ot_ss.at[to], ot_rs.at[me], blk, to)

    def ot_arrival(src):
        return remote(out_send.at[src], out_recv.at[src], ot_ss.at[src], ot_rs.at[src], blk, src)

    barrier = pltpu.get_barrier_semaphore()

    def greet(t, c):
        pl.semaphore_signal(barrier, inc=1, device_id={"head": peer(t)}, device_id_type=MESH)
        return c

    lax.fori_loop(1, n, greet, 0)
    pl.semaphore_signal(barrier, inc=1, device_id={"blk": before}, device_id_type=MESH)
    pl.semaphore_signal(barrier, inc=1, device_id={"blk": after}, device_id_type=MESH)

    def pack(a_ref, b_ref, to_ref, scale):
        for p in range(n // 2):
            cols = slice(2 * HD * p, 2 * HD * (p + 1))
            a, b = a_ref[:, cols], b_ref[:, cols]
            if scale is not None:
                a = (a.astype(F32) * scale).astype(BF16)
            to_ref[2 * p] = jnp.concatenate([a[:, :HD], b[:, :HD]], axis=1)
            to_ref[2 * p + 1] = jnp.concatenate([a[:, HD:], b[:, HD:]], axis=1)

    pack(k_ref, v_ref, kv_send, None)
    kv_win[n + me] = kv_send[me]
    pl.semaphore_wait(barrier, n + 1)

    def send_kv(t, c):
        kv_copy(peer(t)).start()
        return c

    lax.fori_loop(1, n, send_kv, 0)
    pack(q_ref, d_ref, qd_send, HD**-0.5)
    qd_all[me] = qd_send[me]

    def send_qd(t, c):
        qd_copy(peer(t)).start()
        return c

    lax.fori_loop(1, n, send_qd, 0)

    def turn(j):
        kt_win[j] = kv_win[j].T[:HD]

    def forward(t, c):
        i = source(t)

        @pl.when(t > 0)
        def _():
            kv_arrival(i).wait_recv()

        fw_copy(0, i).start()
        fw_copy(1, i).start()
        turn(n + i)
        return c

    lax.fori_loop(0, n, forward, 0)

    def window(t, c):
        i = source(t)
        fw_copy(0, i).wait_recv()
        turn(i)
        fw_copy(1, i).wait_recv()
        turn(2 * n + i)
        return c

    lax.fori_loop(0, n, window, 0)

    lane = lax.broadcasted_iota(jnp.int32, (QB, 2 * HD), 1)

    def fold(x, op):
        return op(x.reshape(QB // 8, 8, QB), axis=0)

    def query(t, c):
        i = source(t)

        @pl.when(t > 0)
        def _():
            qd_arrival(i).wait_recv()

        qd = qd_all[i]
        zero = jnp.zeros_like(qd)
        qd2 = jnp.concatenate([jnp.where(lane < HD, qd, zero), jnp.where(lane < HD, zero, qd)], axis=0)
        ids = [meta[i * NNB + s] for s in range(NNB)]
        top = None
        for s in range(NNB):
            r = lax.dot_general(
                kv_win[ids[s]], qd2, (((1,), (1,)), ((), ())), preferred_element_type=F32
            )
            st[s] = r
            m = fold(r[:, :QB], jnp.max)
            top = m if top is None else jnp.maximum(top, m)
        top = jnp.max(top, axis=0, keepdims=True)
        total = jnp.zeros((8, QB), F32)
        delta = jnp.zeros((8, QB), F32)
        for s in range(NNB):
            e = jnp.exp(st[s, :, :QB] - top)
            total += fold(e, jnp.sum)
            delta += fold(e * st[s, :, QB:], jnp.sum)
            st[s, :, :QB] = e
        inv = 1.0 / jnp.sum(total, axis=0, keepdims=True)
        delta = jnp.sum(delta, axis=0, keepdims=True) * inv
        for s in range(NNB):
            p = st[s, :, :QB] * inv
            ds = p * (st[s, :, QB:] - delta)
            w[s * QB : (s + 1) * QB, :QB] = ds.astype(BF16)
            w[s * QB : (s + 1) * QB, QB:] = p.astype(BF16)
        dqt = jnp.zeros((HD, QB), F32)
        for s in range(0, NNB, 2):
            kt = jnp.concatenate([kt_win[ids[s]], kt_win[ids[s + 1]]], axis=1)
            dqt += jnp.dot(kt, w[s * QB : (s + 2) * QB, :QB], preferred_element_type=F32)
        dqt = (dqt * HD**-0.5).astype(BF16)
        dq_send[i] = dqt

        @pl.when(t > 0)
        def _():
            dq_copy(i).start()

        @pl.when(t == 0)
        def _():
            dq_recv[pl.ds(pl.multiple_of(me * HD, HD), HD)] = dqt

        for s in range(NNB):
            parts[i * NNB + s] = jnp.dot(
                w[s * QB : (s + 1) * QB, :], qd2, preferred_element_type=F32
            )
        return c

    lax.fori_loop(0, n, query, 0)

    def add(e, acc):
        x = parts[meta[at_order + e]]
        acc = x + jnp.where(meta[at_keep + e] > 0, acc, 0.0)
        run[e] = acc
        return acc

    lax.fori_loop(0, pairs, add, jnp.zeros((QB, 2 * HD), F32))

    def summed(j):
        return jnp.where(meta[at_has + j] > 0, run[meta[at_last + j]], 0.0)

    def share(t, c):
        i = peer(t)
        part_send[0, i] = summed(i).astype(BF16)
        pt_copy(0, i).start()
        part_send[1, i] = summed(2 * n + i).astype(BF16)
        pt_copy(1, i).start()
        return c

    lax.fori_loop(1, n + 1, share, 0)

    def gather_dq(t, c):
        dq_arrival(source(t)).wait_recv()
        return c

    lax.fori_loop(1, n, gather_dq, 0)
    for p in range(n // 2):
        cols = slice(2 * HD * p, 2 * HD * (p + 1))
        gq_ref[:, cols] = dq_recv[cols].T

    def home(t, c):
        i = peer(t)
        pt_copy(0, i).wait_recv()
        pt_copy(1, i).wait_recv()
        x = summed(n + i) + part_recv[0, i].astype(F32) + part_recv[1, i].astype(F32)
        out_send[i] = x.astype(BF16)

        @pl.when(t < n)
        def _():
            ot_copy(i).start()

        @pl.when(t == n)
        def _():
            out_recv[me] = x.astype(BF16)

        return c

    lax.fori_loop(1, n + 1, home, 0)

    def gather_out(t, c):
        ot_arrival(source(t)).wait_recv()
        return c

    lax.fori_loop(1, n, gather_out, 0)
    for p in range(n // 2):
        cols = slice(2 * HD * p, 2 * HD * (p + 1))
        a, b = out_recv[2 * p], out_recv[2 * p + 1]
        gk_ref[:, cols] = jnp.concatenate([a[:, :HD], b[:, :HD]], axis=1)
        gv_ref[:, cols] = jnp.concatenate([a[:, HD:], b[:, HD:]], axis=1)

    def drain(t, c):
        to = peer(t)
        kv_copy(to).wait_send()
        qd_copy(to).wait_send()
        dq_copy(to).wait_send()
        ot_copy(to).wait_send()
        return c

    lax.fori_loop(1, n, drain, 0)

    def drain_sides(i, c):
        for side in (0, 1):
            fw_copy(side, i).wait_send()
            pt_copy(side, i).wait_send()
        return c

    lax.fori_loop(0, n, drain_sides, 0)


def per_device(query_rows, key_rows, value_rows, out_grad, block_pairs):
    n = lax.axis_size("head")
    pairs = n * NNB
    place = lax.axis_index("blk")
    own = lax.dynamic_slice_in_dim(block_pairs, place * n, n, 0).reshape(pairs)
    ids = (own - (place - 1) * n) % (n * lax.axis_size("blk"))
    e = jnp.arange(pairs, dtype=jnp.int32)
    less = (ids[None, :] < ids[:, None]) | ((ids[None, :] == ids[:, None]) & (e[None, :] < e[:, None]))
    rank = jnp.sum(less.astype(jnp.int32), axis=1)
    at = rank[None, :] == e[:, None]
    order = jnp.sum(jnp.where(at, e[None, :], 0), axis=1)
    same = (ids[None, :] == ids[:, None]) & (e[None, :] < e[:, None])
    going_on = jnp.any(same, axis=1).astype(jnp.int32)
    keep = jnp.sum(jnp.where(at, going_on[None, :], 0), axis=1)
    j = jnp.arange(3 * n, dtype=jnp.int32)
    upto = jnp.sum((ids[None, :] <= j[:, None]).astype(jnp.int32), axis=1)
    has = jnp.any(ids[None, :] == j[:, None], axis=1).astype(jnp.int32)
    meta = jnp.concatenate([ids, order, keep, jnp.maximum(upto - 1, 0), has]).astype(jnp.int32)

    rows = jax.ShapeDtypeStruct((QB, n * HD), BF16)
    tile = (QB, 2 * HD)
    dma = pltpu.SemaphoreType.DMA
    vmem = pl.BlockSpec(memory_space=pltpu.VMEM)
    return pl.pallas_call(
        functools.partial(kernel, n),
        out_shape=(rows, rows, rows),
        in_specs=[pl.BlockSpec(memory_space=pltpu.SMEM)] + [vmem] * 4,
        out_specs=(vmem, vmem, vmem),
        scratch_shapes=[
            pltpu.VMEM((n,) + tile, BF16),
            pltpu.VMEM((n,) + tile, BF16),
            pltpu.VMEM((3 * n,) + tile, BF16),
            pltpu.VMEM((3 * n, HD, QB), BF16),
            pltpu.VMEM((n,) + tile, BF16),
            pltpu.VMEM((NNB, QB, 2 * QB), F32),
            pltpu.VMEM((NNB * QB, 2 * QB), BF16),
            pltpu.VMEM((pairs,) + tile, F32),
            pltpu.VMEM((pairs,) + tile, F32),
            pltpu.VMEM((n, HD, QB), BF16),
            pltpu.VMEM((n * HD, QB), BF16),
            pltpu.VMEM((2, n) + tile, BF16),
            pltpu.VMEM((2, n) + tile, BF16),
            pltpu.VMEM((n,) + tile, BF16),
            pltpu.VMEM((n,) + tile, BF16),
            dma((n,)),
            dma((n,)),
            dma((2, n)),
            dma((2, n)),
            dma((n,)),
            dma((n,)),
            dma((n,)),
            dma((n,)),
            dma((2, n)),
            dma((2, n)),
            dma((n,)),
            dma((n,)),
        ],
        compiler_params=pltpu.CompilerParams(
            collective_id=0, has_side_effects=True, vmem_limit_bytes=48 * 1024 * 1024
        ),
    )(meta, query_rows, key_rows, value_rows, out_grad)


def solution(mesh):
    rows = P(("blk", "head"), None)
    return jax.shard_map(
        per_device,
        mesh=mesh,
        in_specs=(rows, rows, rows, rows, P()),
        out_specs=(rows, rows, rows),
        check_vma=False,
    )
```

```python
import functools

import jax
import jax.numpy as jnp
from jax import lax
from jax.experimental import pallas as pl
from jax.experimental.pallas import tpu as pltpu
from jax.sharding import PartitionSpec as P

HD = 64
QB = 128
NNB = 8
MESH = pl.DeviceIdType.MESH
BF16 = jnp.bfloat16
F32 = jnp.float32


def kernel(
    n,
    meta,
    q_hbm,
    k_hbm,
    v_hbm,
    d_hbm,
    gq_ref,
    gk_ref,
    gv_ref,
    q_ref,
    k_ref,
    v_ref,
    d_ref,
    kv_send,
    qd_send,
    kv_win,
    kt_win,
    qd_all,
    st0,
    st1,
    tops0,
    tops1,
    w0,
    w1,
    parts,
    run,
    dq_send,
    dq_recv,
    part_send,
    part_recv,
    out_send,
    out_recv,
    in_sems,
    kv_ss,
    kv_rs,
    fw_ss,
    fw_rs,
    qd_ss,
    qd_rs,
    dq_ss,
    dq_rs,
    pt_ss,
    pt_rs,
    ot_ss,
    ot_rs,
):
    blk, me = lax.axis_index("blk"), lax.axis_index("head")
    nblk = lax.axis_size("blk")
    before, after = lax.rem(blk + nblk - 1, nblk), lax.rem(blk + 1, nblk)
    pairs = n * NNB
    at_order, at_keep, at_last, at_has = pairs, 2 * pairs, 3 * pairs, 3 * pairs + 3 * n
    nz = n // 2
    my_y, my_z = me // nz, lax.rem(me, nz)

    def offset(t):
        k = t // 2
        return lax.rem(t, 2), (k + 1) // 2 * (2 * lax.rem(k, 2) - 1)

    def peer(t):
        dy, dz = offset(t)
        return lax.rem(my_y + dy, 2) * nz + lax.rem(my_z + dz + nz, nz)

    def source(t):
        dy, dz = offset(t)
        return lax.rem(my_y + dy, 2) * nz + lax.rem(my_z - dz + nz, nz)

    def remote(src, dst, ss, rs, b, h):
        return pltpu.make_async_remote_copy(
            src_ref=src, dst_ref=dst, send_sem=ss, recv_sem=rs, device_id={"blk": b, "head": h}, device_id_type=MESH
        )

    def kv_copy(to):
        return remote(kv_send.at[to], kv_win.at[n + me], kv_ss.at[to], kv_rs.at[me], blk, to)

    def kv_arrival(src):
        return remote(kv_send.at[src], kv_win.at[n + src], kv_ss.at[src], kv_rs.at[src], blk, src)

    def qd_copy(to):
        return remote(qd_send.at[to], qd_all.at[me], qd_ss.at[to], qd_rs.at[me], blk, to)

    def qd_arrival(src):
        return remote(qd_send.at[src], qd_all.at[src], qd_ss.at[src], qd_rs.at[src], blk, src)

    def fw_copy(side, i):
        dst = kv_win.at[i] if side == 0 else kv_win.at[2 * n + i]
        return remote(
            kv_win.at[n + i], dst, fw_ss.at[side, i], fw_rs.at[side, i], after if side == 0 else before, me
        )

    def pt_copy(side, i):
        return remote(
            part_send.at[side, i],
            part_recv.at[side, i],
            pt_ss.at[side, i],
            pt_rs.at[side, i],
            before if side == 0 else after,
            me,
        )

    def dq_copy(to):
        rows = pl.ds(pl.multiple_of(me * HD, HD), HD)
        return remote(dq_send.at[to], dq_recv.at[rows], dq_ss.at[to], dq_rs.at[me], blk, to)

    def dq_arrival(src):
        rows = pl.ds(pl.multiple_of(src * HD, HD), HD)
        return remote(dq_send.at[src], dq_recv.at[rows], dq_ss.at[src], dq_rs.at[src], blk, src)

    def ot_copy(to):
        return remote(out_send.at[to], out_recv.at[me], ot_ss.at[to], ot_rs.at[me], blk, to)

    def ot_arrival(src):
        return remote(out_send.at[src], out_recv.at[src], ot_ss.at[src], ot_rs.at[src], blk, src)

    def read(i):
        src, dst = (k_hbm, v_hbm, q_hbm, d_hbm)[i], (k_ref, v_ref, q_ref, d_ref)[i]
        return pltpu.make_async_copy(src, dst, in_sems.at[i])

    barrier = pltpu.get_barrier_semaphore()

    def greet(t, c):
        pl.semaphore_signal(barrier, inc=1, device_id={"head": peer(t)}, device_id_type=MESH)
        return c

    lax.fori_loop(1, n, greet, 0)
    pl.semaphore_signal(barrier, inc=1, device_id={"blk": before}, device_id_type=MESH)
    pl.semaphore_signal(barrier, inc=1, device_id={"blk": after}, device_id_type=MESH)
    for i in range(4):
        read(i).start()

    def pack(a_ref, b_ref, to_ref, scale):
        for p in range(n // 2):
            cols = slice(2 * HD * p, 2 * HD * (p + 1))
            a, b = a_ref[:, cols], b_ref[:, cols]
            if scale is not None:
                a = (a.astype(F32) * scale).astype(BF16)
            to_ref[2 * p] = jnp.concatenate([a[:, :HD], b[:, :HD]], axis=1)
            to_ref[2 * p + 1] = jnp.concatenate([a[:, HD:], b[:, HD:]], axis=1)

    read(0).wait()
    read(1).wait()
    pack(k_ref, v_ref, kv_send, None)
    kv_win[n + me] = kv_send[me]
    pl.semaphore_wait(barrier, n + 1)

    def send_kv(t, c):
        kv_copy(peer(t)).start()
        return c

    lax.fori_loop(1, n, send_kv, 0)
    read(2).wait()
    read(3).wait()
    pack(q_ref, d_ref, qd_send, HD**-0.5)
    qd_all[me] = qd_send[me]

    def turn(j):
        kt_win[j] = kv_win[j].T[:HD]

    def forward(t, c):
        i = source(t)

        @pl.when(t > 0)
        def _():
            kv_arrival(i).wait_recv()
            qd_copy(peer(t)).start()

        fw_copy(0, i).start()
        fw_copy(1, i).start()
        turn(n + i)
        return c

    lax.fori_loop(0, n, forward, 0)

    def window(t, c):
        i = source(t)
        fw_copy(0, i).wait_recv()
        turn(i)
        fw_copy(1, i).wait_recv()
        turn(2 * n + i)
        return c

    lax.fori_loop(0, n, window, 0)

    lane = lax.broadcasted_iota(jnp.int32, (QB, 2 * HD), 1)

    def fold(x, op):
        return op(x.reshape(QB // 8, 8, QB), axis=0)

    def operands(i):
        qd = qd_all[i]
        zero = jnp.zeros_like(qd)
        qd2 = jnp.concatenate([jnp.where(lane < HD, qd, zero), jnp.where(lane < HD, zero, qd)], axis=0)
        return qd2, [meta[i * NNB + s] for s in range(NNB)]

    def scores(i, st, tops):
        qd2, ids = operands(i)
        top = None
        for s in range(NNB):
            r = lax.dot_general(
                kv_win[ids[s]], qd2, (((1,), (1,)), ((), ())), preferred_element_type=F32
            )
            st[s] = r
            m = fold(r[:, :QB], jnp.max)
            top = m if top is None else jnp.maximum(top, m)
        tops[...] = top

    def grads(i, st, tops, w):
        qd2, ids = operands(i)
        top = jnp.max(tops[...], axis=0, keepdims=True)
        total = jnp.zeros((8, QB), F32)
        delta = jnp.zeros((8, QB), F32)
        for s in range(NNB):
            e = jnp.exp(st[s, :, :QB] - top)
            total += fold(e, jnp.sum)
            delta += fold(e * st[s, :, QB:], jnp.sum)
            st[s, :, :QB] = e
        inv = 1.0 / jnp.sum(total, axis=0, keepdims=True)
        delta = jnp.sum(delta, axis=0, keepdims=True) * inv
        for s in range(NNB):
            p = st[s, :, :QB] * inv
            ds = p * (st[s, :, QB:] - delta)
            w[s * QB : (s + 1) * QB, :QB] = ds.astype(BF16)
            w[s * QB : (s + 1) * QB, QB:] = p.astype(BF16)
        dqt = jnp.zeros((HD, QB), F32)
        for s in range(0, NNB, 2):
            kt = jnp.concatenate([kt_win[ids[s]], kt_win[ids[s + 1]]], axis=1)
            dqt += jnp.dot(kt, w[s * QB : (s + 2) * QB, :QB], preferred_element_type=F32)
        dq_send[i] = (dqt * HD**-0.5).astype(BF16)
        for s in range(NNB):
            parts[i * NNB + s] = jnp.dot(
                w[s * QB : (s + 1) * QB, :], qd2, preferred_element_type=F32
            )

    scores(me, st0, tops0)

    def query(u, c):
        i0, i1, i2 = source(2 * u), source(2 * u + 1), source(lax.rem(2 * u + 2, n))
        qd_arrival(i1).wait_recv()

        @pl.when(2 * u + 2 < n)
        def _():
            qd_arrival(i2).wait_recv()

        scores(i1, st1, tops1)
        grads(i0, st0, tops0, w0)
        scores(i2, st0, tops0)
        grads(i1, st1, tops1, w1)

        @pl.when(u > 0)
        def _():
            dq_copy(i0).start()

        dq_copy(i1).start()
        return c

    lax.fori_loop(0, n // 2, query, 0)
    dq_recv[pl.ds(pl.multiple_of(me * HD, HD), HD)] = dq_send[me]

    def add(e, acc):
        x = parts[meta[at_order + e]]
        acc = x + jnp.where(meta[at_keep + e] > 0, acc, 0.0)
        run[e] = acc
        return acc

    lax.fori_loop(0, pairs, add, jnp.zeros((QB, 2 * HD), F32))

    def summed(j):
        return jnp.where(meta[at_has + j] > 0, run[meta[at_last + j]], 0.0)

    def share(t, c):
        i = peer(n - t)
        part_send[0, i] = summed(i).astype(BF16)
        pt_copy(0, i).start()
        part_send[1, i] = summed(2 * n + i).astype(BF16)
        pt_copy(1, i).start()
        return c

    lax.fori_loop(1, n + 1, share, 0)

    def gather_dq(t, c):
        dq_arrival(source(t)).wait_recv()
        return c

    lax.fori_loop(1, n, gather_dq, 0)
    for p in range(n // 2):
        cols = slice(2 * HD * p, 2 * HD * (p + 1))
        gq_ref[:, cols] = dq_recv[cols].T

    def home(t, c):
        i = peer(n - t)
        pt_copy(0, i).wait_recv()
        pt_copy(1, i).wait_recv()
        x = summed(n + i) + part_recv[0, i].astype(F32) + part_recv[1, i].astype(F32)
        out_send[i] = x.astype(BF16)

        @pl.when(t < n)
        def _():
            ot_copy(i).start()

        @pl.when(t == n)
        def _():
            out_recv[me] = x.astype(BF16)

        return c

    lax.fori_loop(1, n + 1, home, 0)

    def gather_out(t, c):
        ot_arrival(source(t)).wait_recv()
        return c

    lax.fori_loop(1, n, gather_out, 0)
    for p in range(n // 2):
        cols = slice(2 * HD * p, 2 * HD * (p + 1))
        a, b = out_recv[2 * p], out_recv[2 * p + 1]
        gk_ref[:, cols] = jnp.concatenate([a[:, :HD], b[:, :HD]], axis=1)
        gv_ref[:, cols] = jnp.concatenate([a[:, HD:], b[:, HD:]], axis=1)

    def drain(t, c):
        to = peer(t)
        kv_copy(to).wait_send()
        qd_copy(to).wait_send()
        dq_copy(to).wait_send()
        ot_copy(to).wait_send()
        return c

    lax.fori_loop(1, n, drain, 0)

    def drain_sides(i, c):
        for side in (0, 1):
            fw_copy(side, i).wait_send()
            pt_copy(side, i).wait_send()
        return c

    lax.fori_loop(0, n, drain_sides, 0)


def per_device(query_rows, key_rows, value_rows, out_grad, block_pairs):
    n = lax.axis_size("head")
    pairs = n * NNB
    place = lax.axis_index("blk")
    own = lax.dynamic_slice_in_dim(block_pairs, place * n, n, 0).reshape(pairs)
    ids = (own - (place - 1) * n) % (n * lax.axis_size("blk"))
    e = jnp.arange(pairs, dtype=jnp.int32)
    less = (ids[None, :] < ids[:, None]) | ((ids[None, :] == ids[:, None]) & (e[None, :] < e[:, None]))
    rank = jnp.sum(less.astype(jnp.int32), axis=1)
    at = rank[None, :] == e[:, None]
    order = jnp.sum(jnp.where(at, e[None, :], 0), axis=1)
    same = (ids[None, :] == ids[:, None]) & (e[None, :] < e[:, None])
    going_on = jnp.any(same, axis=1).astype(jnp.int32)
    keep = jnp.sum(jnp.where(at, going_on[None, :], 0), axis=1)
    j = jnp.arange(3 * n, dtype=jnp.int32)
    upto = jnp.sum((ids[None, :] <= j[:, None]).astype(jnp.int32), axis=1)
    has = jnp.any(ids[None, :] == j[:, None], axis=1).astype(jnp.int32)
    meta = jnp.concatenate([ids, order, keep, jnp.maximum(upto - 1, 0), has]).astype(jnp.int32)

    rows = jax.ShapeDtypeStruct((QB, n * HD), BF16)
    tile = (QB, 2 * HD)
    dma = pltpu.SemaphoreType.DMA
    vmem = pl.BlockSpec(memory_space=pltpu.VMEM)
    return pl.pallas_call(
        functools.partial(kernel, n),
        out_shape=(rows, rows, rows),
        in_specs=[pl.BlockSpec(memory_space=pltpu.SMEM)] + [pl.BlockSpec(memory_space=pl.ANY)] * 4,
        out_specs=(vmem, vmem, vmem),
        scratch_shapes=[
            pltpu.VMEM((QB, n * HD), BF16),
            pltpu.VMEM((QB, n * HD), BF16),
            pltpu.VMEM((QB, n * HD), BF16),
            pltpu.VMEM((QB, n * HD), BF16),
            pltpu.VMEM((n,) + tile, BF16),
            pltpu.VMEM((n,) + tile, BF16),
            pltpu.VMEM((3 * n,) + tile, BF16),
            pltpu.VMEM((3 * n, HD, QB), BF16),
            pltpu.VMEM((n,) + tile, BF16),
            pltpu.VMEM((NNB, QB, 2 * QB), F32),
            pltpu.VMEM((NNB, QB, 2 * QB), F32),
            pltpu.VMEM((8, QB), F32),
            pltpu.VMEM((8, QB), F32),
            pltpu.VMEM((NNB * QB, 2 * QB), BF16),
            pltpu.VMEM((NNB * QB, 2 * QB), BF16),
            pltpu.VMEM((pairs,) + tile, F32),
            pltpu.VMEM((pairs,) + tile, F32),
            pltpu.VMEM((n, HD, QB), BF16),
            pltpu.VMEM((n * HD, QB), BF16),
            pltpu.VMEM((2, n) + tile, BF16),
            pltpu.VMEM((2, n) + tile, BF16),
            pltpu.VMEM((n,) + tile, BF16),
            pltpu.VMEM((n,) + tile, BF16),
            dma((4,)),
            dma((n,)),
            dma((n,)),
            dma((2, n)),
            dma((2, n)),
            dma((n,)),
            dma((n,)),
            dma((n,)),
            dma((n,)),
            dma((2, n)),
            dma((2, n)),
            dma((n,)),
            dma((n,)),
        ],
        compiler_params=pltpu.CompilerParams(
            collective_id=0, has_side_effects=True, vmem_limit_bytes=60 * 1024 * 1024
        ),
    )(meta, query_rows, key_rows, value_rows, out_grad)


def solution(mesh):
    rows = P(("blk", "head"), None)
    return jax.shard_map(
        per_device,
        mesh=mesh,
        in_specs=(rows, rows, rows, rows, P()),
        out_specs=(rows, rows, rows),
        check_vma=False,
    )
```

```python
import functools

import jax
import jax.numpy as jnp
from jax import lax
from jax.experimental import pallas as pl
from jax.experimental.pallas import tpu as pltpu
from jax.sharding import PartitionSpec as P

HD = 64
QB = 128
NNB = 8
MESH = pl.DeviceIdType.MESH
BF16 = jnp.bfloat16
F32 = jnp.float32


def kernel(
    n,
    meta,
    q_hbm,
    k_hbm,
    v_hbm,
    d_hbm,
    dq_recv,
    out_recv,
    q_ref,
    k_ref,
    v_ref,
    d_ref,
    kv_send,
    qd_send,
    kv_win,
    kt_win,
    qd_all,
    st0,
    st1,
    tops0,
    tops1,
    w0,
    w1,
    parts,
    run,
    dq_send,
    part_send,
    part_recv,
    out_send,
    in_sems,
    kv_ss,
    kv_rs,
    fw_ss,
    fw_rs,
    qd_ss,
    qd_rs,
    dq_ss,
    dq_rs,
    pt_ss,
    pt_rs,
    ot_ss,
    ot_rs,
):
    blk, me = lax.axis_index("blk"), lax.axis_index("head")
    nblk = lax.axis_size("blk")
    before, after = lax.rem(blk + nblk - 1, nblk), lax.rem(blk + 1, nblk)
    pairs = n * NNB
    at_order, at_keep, at_last, at_has = pairs, 2 * pairs, 3 * pairs, 3 * pairs + 3 * n
    nz = n // 2
    my_y, my_z = me // nz, lax.rem(me, nz)

    def offset(t):
        k = t // 2
        return lax.rem(t, 2), (k + 1) // 2 * (2 * lax.rem(k, 2) - 1)

    def peer(t):
        dy, dz = offset(t)
        return lax.rem(my_y + dy, 2) * nz + lax.rem(my_z + dz + nz, nz)

    def source(t):
        dy, dz = offset(t)
        return lax.rem(my_y + dy, 2) * nz + lax.rem(my_z - dz + nz, nz)

    def remote(src, dst, ss, rs, b, h):
        return pltpu.make_async_remote_copy(
            src_ref=src, dst_ref=dst, send_sem=ss, recv_sem=rs, device_id={"blk": b, "head": h}, device_id_type=MESH
        )

    def kv_copy(to):
        return remote(kv_send.at[to], kv_win.at[n + me], kv_ss.at[to], kv_rs.at[me], blk, to)

    def kv_arrival(src):
        return remote(kv_send.at[src], kv_win.at[n + src], kv_ss.at[src], kv_rs.at[src], blk, src)

    def qd_copy(to):
        return remote(qd_send.at[to], qd_all.at[me], qd_ss.at[to], qd_rs.at[me], blk, to)

    def qd_arrival(src):
        return remote(qd_send.at[src], qd_all.at[src], qd_ss.at[src], qd_rs.at[src], blk, src)

    def fw_copy(side, i):
        dst = kv_win.at[i] if side == 0 else kv_win.at[2 * n + i]
        return remote(
            kv_win.at[n + i], dst, fw_ss.at[side, i], fw_rs.at[side, i], after if side == 0 else before, me
        )

    def pt_copy(side, i):
        return remote(
            part_send.at[side, i],
            part_recv.at[side, i],
            pt_ss.at[side, i],
            pt_rs.at[side, i],
            before if side == 0 else after,
            me,
        )

    def dq_copy(to):
        rows = pl.ds(pl.multiple_of(me * HD, HD), HD)
        return remote(dq_send.at[to], dq_recv.at[rows], dq_ss.at[to], dq_rs.at[me], blk, to)

    def dq_arrival(src):
        rows = pl.ds(pl.multiple_of(src * HD, HD), HD)
        return remote(dq_send.at[src], dq_recv.at[rows], dq_ss.at[src], dq_rs.at[src], blk, src)

    def ot_copy(to):
        return remote(out_send.at[to], out_recv.at[me], ot_ss.at[to], ot_rs.at[me], blk, to)

    def ot_arrival(src):
        return remote(out_send.at[src], out_recv.at[src], ot_ss.at[src], ot_rs.at[src], blk, src)

    def read(i):
        src, dst = (k_hbm, v_hbm, q_hbm, d_hbm)[i], (k_ref, v_ref, q_ref, d_ref)[i]
        return pltpu.make_async_copy(src, dst, in_sems.at[i])

    barrier = pltpu.get_barrier_semaphore()

    def greet(t, c):
        pl.semaphore_signal(barrier, inc=1, device_id={"head": peer(t)}, device_id_type=MESH)
        return c

    lax.fori_loop(1, n, greet, 0)
    pl.semaphore_signal(barrier, inc=1, device_id={"blk": before}, device_id_type=MESH)
    pl.semaphore_signal(barrier, inc=1, device_id={"blk": after}, device_id_type=MESH)
    for i in range(4):
        read(i).start()

    def pack(a_ref, b_ref, to_ref, scale):
        for p in range(n // 2):
            cols = slice(2 * HD * p, 2 * HD * (p + 1))
            a, b = a_ref[:, cols], b_ref[:, cols]
            if scale is not None:
                a = (a.astype(F32) * scale).astype(BF16)
            to_ref[2 * p] = jnp.concatenate([a[:, :HD], b[:, :HD]], axis=1)
            to_ref[2 * p + 1] = jnp.concatenate([a[:, HD:], b[:, HD:]], axis=1)

    read(0).wait()
    read(1).wait()
    pack(k_ref, v_ref, kv_send, None)
    kv_win[n + me] = kv_send[me]
    pl.semaphore_wait(barrier, n + 1)

    def send_kv(t, c):
        kv_copy(peer(t)).start()
        return c

    lax.fori_loop(1, n, send_kv, 0)
    read(2).wait()
    read(3).wait()
    pack(q_ref, d_ref, qd_send, HD**-0.5)
    qd_all[me] = qd_send[me]

    def turn(j):
        kt_win[j] = kv_win[j].T[:HD]

    def forward(t, c):
        i = source(t)

        @pl.when(t > 0)
        def _():
            kv_arrival(i).wait_recv()

        fw_copy(0, i).start()
        fw_copy(1, i).start()
        turn(n + i)
        return c

    lax.fori_loop(0, n, forward, 0)

    def send_qd(t, c):
        qd_copy(peer(t)).start()
        return c

    lax.fori_loop(1, n, send_qd, 0)

    def window(t, c):
        i = source(t)
        fw_copy(0, i).wait_recv()
        turn(i)
        fw_copy(1, i).wait_recv()
        turn(2 * n + i)
        return c

    lax.fori_loop(0, n, window, 0)

    lane = lax.broadcasted_iota(jnp.int32, (QB, 2 * HD), 1)

    def fold(x, op):
        return op(x.reshape(QB // 8, 8, QB), axis=0)

    def operands(i):
        qd = qd_all[i]
        zero = jnp.zeros_like(qd)
        qd2 = jnp.concatenate([jnp.where(lane < HD, qd, zero), jnp.where(lane < HD, zero, qd)], axis=0)
        return qd2, [meta[i * NNB + s] for s in range(NNB)]

    def scores(i, st, tops):
        qd2, ids = operands(i)
        top = None
        for s in range(NNB):
            r = lax.dot_general(
                kv_win[ids[s]], qd2, (((1,), (1,)), ((), ())), preferred_element_type=F32
            )
            st[s] = r
            m = fold(r[:, :QB], jnp.max)
            top = m if top is None else jnp.maximum(top, m)
        tops[...] = top

    def grads(i, st, tops, w):
        qd2, ids = operands(i)
        top = jnp.max(tops[...], axis=0, keepdims=True)
        total = jnp.zeros((8, QB), F32)
        delta = jnp.zeros((8, QB), F32)
        for s in range(NNB):
            e = jnp.exp(st[s, :, :QB] - top)
            total += fold(e, jnp.sum)
            delta += fold(e * st[s, :, QB:], jnp.sum)
            st[s, :, :QB] = e
        inv = 1.0 / jnp.sum(total, axis=0, keepdims=True)
        delta = jnp.sum(delta, axis=0, keepdims=True) * inv
        for s in range(NNB):
            p = st[s, :, :QB] * inv
            ds = p * (st[s, :, QB:] - delta)
            w[s * QB : (s + 1) * QB, :QB] = ds.astype(BF16)
            w[s * QB : (s + 1) * QB, QB:] = p.astype(BF16)
        dqt = jnp.zeros((HD, QB), F32)
        for s in range(0, NNB, 2):
            kt = jnp.concatenate([kt_win[ids[s]], kt_win[ids[s + 1]]], axis=1)
            dqt += jnp.dot(kt, w[s * QB : (s + 2) * QB, :QB], preferred_element_type=F32)
        dq_send[i] = (dqt * HD**-0.5).astype(BF16)
        for s in range(NNB):
            parts[i * NNB + s] = jnp.dot(
                w[s * QB : (s + 1) * QB, :], qd2, preferred_element_type=F32
            )

    scores(me, st0, tops0)

    def query(u, c):
        i0, i1, i2 = source(2 * u), source(2 * u + 1), source(lax.rem(2 * u + 2, n))
        qd_arrival(i1).wait_recv()

        @pl.when(2 * u + 2 < n)
        def _():
            qd_arrival(i2).wait_recv()

        scores(i1, st1, tops1)
        grads(i0, st0, tops0, w0)
        scores(i2, st0, tops0)
        grads(i1, st1, tops1, w1)

        @pl.when(u > 0)
        def _():
            dq_copy(i0).start()

        dq_copy(i1).start()
        return c

    lax.fori_loop(0, n // 2, query, 0)
    dq_recv[pl.ds(pl.multiple_of(me * HD, HD), HD)] = dq_send[me]

    def add(e, acc):
        x = parts[meta[at_order + e]]
        acc = x + jnp.where(meta[at_keep + e] > 0, acc, 0.0)
        run[e] = acc
        return acc

    lax.fori_loop(0, pairs, add, jnp.zeros((QB, 2 * HD), F32))

    def summed(j):
        return jnp.where(meta[at_has + j] > 0, run[meta[at_last + j]], 0.0)

    def share(t, c):
        i = peer(n - t)
        part_send[0, i] = summed(i).astype(BF16)
        pt_copy(0, i).start()
        part_send[1, i] = summed(2 * n + i).astype(BF16)
        pt_copy(1, i).start()
        return c

    lax.fori_loop(1, n + 1, share, 0)

    def gather_dq(t, c):
        dq_arrival(source(t)).wait_recv()
        return c

    lax.fori_loop(1, n, gather_dq, 0)

    def home(t, c):
        i = peer(n - t)
        pt_copy(0, i).wait_recv()
        pt_copy(1, i).wait_recv()
        x = summed(n + i) + part_recv[0, i].astype(F32) + part_recv[1, i].astype(F32)
        out_send[i] = x.astype(BF16)

        @pl.when(t < n)
        def _():
            ot_copy(i).start()

        @pl.when(t == n)
        def _():
            out_recv[me] = x.astype(BF16)

        return c

    lax.fori_loop(1, n + 1, home, 0)

    def gather_out(t, c):
        ot_arrival(source(t)).wait_recv()
        return c

    lax.fori_loop(1, n, gather_out, 0)

    def drain(t, c):
        to = peer(t)
        kv_copy(to).wait_send()
        qd_copy(to).wait_send()
        dq_copy(to).wait_send()
        ot_copy(to).wait_send()
        return c

    lax.fori_loop(1, n, drain, 0)

    def drain_sides(i, c):
        for side in (0, 1):
            fw_copy(side, i).wait_send()
            pt_copy(side, i).wait_send()
        return c

    lax.fori_loop(0, n, drain_sides, 0)


def unpack(n, dq_ref, out_ref, gq_ref, gk_ref, gv_ref):
    for p in range(n // 2):
        cols = slice(2 * HD * p, 2 * HD * (p + 1))
        gq_ref[:, cols] = dq_ref[cols].T
        a, b = out_ref[2 * p], out_ref[2 * p + 1]
        gk_ref[:, cols] = jnp.concatenate([a[:, :HD], b[:, :HD]], axis=1)
        gv_ref[:, cols] = jnp.concatenate([a[:, HD:], b[:, HD:]], axis=1)


def per_device(query_rows, key_rows, value_rows, out_grad, block_pairs):
    n = lax.axis_size("head")
    pairs = n * NNB
    place = lax.axis_index("blk")
    own = lax.dynamic_slice_in_dim(block_pairs, place * n, n, 0).reshape(pairs)
    ids = (own - (place - 1) * n) % (n * lax.axis_size("blk"))
    e = jnp.arange(pairs, dtype=jnp.int32)
    less = (ids[None, :] < ids[:, None]) | ((ids[None, :] == ids[:, None]) & (e[None, :] < e[:, None]))
    rank = jnp.sum(less.astype(jnp.int32), axis=1)
    at = rank[None, :] == e[:, None]
    order = jnp.sum(jnp.where(at, e[None, :], 0), axis=1)
    same = (ids[None, :] == ids[:, None]) & (e[None, :] < e[:, None])
    going_on = jnp.any(same, axis=1).astype(jnp.int32)
    keep = jnp.sum(jnp.where(at, going_on[None, :], 0), axis=1)
    j = jnp.arange(3 * n, dtype=jnp.int32)
    upto = jnp.sum((ids[None, :] <= j[:, None]).astype(jnp.int32), axis=1)
    has = jnp.any(ids[None, :] == j[:, None], axis=1).astype(jnp.int32)
    meta = jnp.concatenate([ids, order, keep, jnp.maximum(upto - 1, 0), has]).astype(jnp.int32)

    rows = jax.ShapeDtypeStruct((QB, n * HD), BF16)
    tile = (QB, 2 * HD)
    dma = pltpu.SemaphoreType.DMA
    vmem = pl.BlockSpec(memory_space=pltpu.VMEM)
    arrived = pl.pallas_call(
        functools.partial(kernel, n),
        out_shape=(
            jax.ShapeDtypeStruct((n * HD, QB), BF16),
            jax.ShapeDtypeStruct((n,) + tile, BF16),
        ),
        in_specs=[pl.BlockSpec(memory_space=pltpu.SMEM)] + [pl.BlockSpec(memory_space=pl.ANY)] * 4,
        out_specs=(vmem, vmem),
        scratch_shapes=[
            pltpu.VMEM((QB, n * HD), BF16),
            pltpu.VMEM((QB, n * HD), BF16),
            pltpu.VMEM((QB, n * HD), BF16),
            pltpu.VMEM((QB, n * HD), BF16),
            pltpu.VMEM((n,) + tile, BF16),
            pltpu.VMEM((n,) + tile, BF16),
            pltpu.VMEM((3 * n,) + tile, BF16),
            pltpu.VMEM((3 * n, HD, QB), BF16),
            pltpu.VMEM((n,) + tile, BF16),
            pltpu.VMEM((NNB, QB, 2 * QB), F32),
            pltpu.VMEM((NNB, QB, 2 * QB), F32),
            pltpu.VMEM((8, QB), F32),
            pltpu.VMEM((8, QB), F32),
            pltpu.VMEM((NNB * QB, 2 * QB), BF16),
            pltpu.VMEM((NNB * QB, 2 * QB), BF16),
            pltpu.VMEM((pairs,) + tile, F32),
            pltpu.VMEM((pairs,) + tile, F32),
            pltpu.VMEM((n, HD, QB), BF16),
            pltpu.VMEM((2, n) + tile, BF16),
            pltpu.VMEM((2, n) + tile, BF16),
            pltpu.VMEM((n,) + tile, BF16),
            dma((4,)),
            dma((n,)),
            dma((n,)),
            dma((2, n)),
            dma((2, n)),
            dma((n,)),
            dma((n,)),
            dma((n,)),
            dma((n,)),
            dma((2, n)),
            dma((2, n)),
            dma((n,)),
            dma((n,)),
        ],
        compiler_params=pltpu.CompilerParams(
            collective_id=0, has_side_effects=True, vmem_limit_bytes=60 * 1024 * 1024
        ),
    )(meta, query_rows, key_rows, value_rows, out_grad)
    return pl.pallas_call(
        functools.partial(unpack, n),
        out_shape=(rows, rows, rows),
        in_specs=[vmem, vmem],
        out_specs=(vmem, vmem, vmem),
    )(*arrived)


def solution(mesh):
    rows = P(("blk", "head"), None)
    return jax.shard_map(
        per_device,
        mesh=mesh,
        in_specs=(rows, rows, rows, rows, P()),
        out_specs=(rows, rows, rows),
        check_vma=False,
    )
```

```python
import functools

import jax
import jax.numpy as jnp
from jax import lax
from jax.experimental import pallas as pl
from jax.experimental.pallas import tpu as pltpu
from jax.sharding import PartitionSpec as P

HD = 64
QB = 128
NNB = 8
MESH = pl.DeviceIdType.MESH
BF16 = jnp.bfloat16
F32 = jnp.float32


def kernel(
    n,
    meta,
    q_hbm,
    k_hbm,
    v_hbm,
    d_hbm,
    dq_recv,
    out_recv,
    q_ref,
    k_ref,
    v_ref,
    d_ref,
    kv_send,
    qd_send,
    kv_win,
    kt_win,
    qd_all,
    st0,
    st1,
    tops0,
    tops1,
    w0,
    w1,
    parts,
    run,
    dq_send,
    part_send,
    part_recv,
    out_send,
    in_sems,
    kv_ss,
    kv_rs,
    fw_ss,
    fw_rs,
    qd_ss,
    qd_rs,
    dq_ss,
    dq_rs,
    pt_ss,
    pt_rs,
    ot_ss,
    ot_rs,
):
    blk, me = lax.axis_index("blk"), lax.axis_index("head")
    nblk = lax.axis_size("blk")
    before, after = lax.rem(blk + nblk - 1, nblk), lax.rem(blk + 1, nblk)
    pairs = n * NNB
    at_order, at_keep, at_last, at_has = pairs, 2 * pairs, 3 * pairs, 3 * pairs + 3 * n
    nz = n // 2
    my_y, my_z = me // nz, lax.rem(me, nz)

    def offset(t):
        k = t // 2
        return lax.rem(t, 2), (k + 1) // 2 * (2 * lax.rem(k, 2) - 1)

    def peer(t):
        dy, dz = offset(t)
        return lax.rem(my_y + dy, 2) * nz + lax.rem(my_z + dz + nz, nz)

    def source(t):
        dy, dz = offset(t)
        return lax.rem(my_y + dy, 2) * nz + lax.rem(my_z - dz + nz, nz)

    def remote(src, dst, ss, rs, b, h):
        return pltpu.make_async_remote_copy(
            src_ref=src, dst_ref=dst, send_sem=ss, recv_sem=rs, device_id={"blk": b, "head": h}, device_id_type=MESH
        )

    def kv_copy(to):
        return remote(kv_send.at[to], kv_win.at[n + me], kv_ss.at[to], kv_rs.at[me], blk, to)

    def kv_arrival(src):
        return remote(kv_send.at[src], kv_win.at[n + src], kv_ss.at[src], kv_rs.at[src], blk, src)

    def qd_copy(to):
        return remote(qd_send.at[to], qd_all.at[me], qd_ss.at[to], qd_rs.at[me], blk, to)

    def qd_arrival(src):
        return remote(qd_send.at[src], qd_all.at[src], qd_ss.at[src], qd_rs.at[src], blk, src)

    def fw_copy(side, i):
        dst = kv_win.at[i] if side == 0 else kv_win.at[2 * n + i]
        return remote(
            kv_win.at[n + i], dst, fw_ss.at[side, i], fw_rs.at[side, i], after if side == 0 else before, me
        )

    def pt_copy(side, i):
        return remote(
            part_send.at[side, i],
            part_recv.at[side, i],
            pt_ss.at[side, i],
            pt_rs.at[side, i],
            before if side == 0 else after,
            me,
        )

    def dq_copy(to):
        rows = pl.ds(pl.multiple_of(me * HD, HD), HD)
        return remote(dq_send.at[to], dq_recv.at[rows], dq_ss.at[to], dq_rs.at[me], blk, to)

    def dq_arrival(src):
        rows = pl.ds(pl.multiple_of(src * HD, HD), HD)
        return remote(dq_send.at[src], dq_recv.at[rows], dq_ss.at[src], dq_rs.at[src], blk, src)

    def ot_copy(to):
        return remote(out_send.at[to], out_recv.at[me], ot_ss.at[to], ot_rs.at[me], blk, to)

    def ot_arrival(src):
        return remote(out_send.at[src], out_recv.at[src], ot_ss.at[src], ot_rs.at[src], blk, src)

    def read(i):
        src, dst = (k_hbm, v_hbm, q_hbm, d_hbm)[i], (k_ref, v_ref, q_ref, d_ref)[i]
        return pltpu.make_async_copy(src, dst, in_sems.at[i])

    barrier = pltpu.get_barrier_semaphore()

    def greet(t, c):
        pl.semaphore_signal(barrier, inc=1, device_id={"head": peer(t)}, device_id_type=MESH)
        return c

    lax.fori_loop(1, n, greet, 0)
    pl.semaphore_signal(barrier, inc=1, device_id={"blk": before}, device_id_type=MESH)
    pl.semaphore_signal(barrier, inc=1, device_id={"blk": after}, device_id_type=MESH)
    for i in range(4):
        read(i).start()

    def pack(a_ref, b_ref, to_ref, scale):
        for p in range(n // 2):
            cols = slice(2 * HD * p, 2 * HD * (p + 1))
            a, b = a_ref[:, cols], b_ref[:, cols]
            if scale is not None:
                a = (a.astype(F32) * scale).astype(BF16)
            to_ref[2 * p] = jnp.concatenate([a[:, :HD], b[:, :HD]], axis=1)
            to_ref[2 * p + 1] = jnp.concatenate([a[:, HD:], b[:, HD:]], axis=1)

    read(0).wait()
    read(1).wait()
    pack(k_ref, v_ref, kv_send, None)
    kv_win[n + me] = kv_send[me]
    pl.semaphore_wait(barrier, n + 1)

    def send_kv(t, c):
        kv_copy(peer(t)).start()
        return c

    lax.fori_loop(1, n, send_kv, 0)
    read(2).wait()
    read(3).wait()
    pack(q_ref, d_ref, qd_send, HD**-0.5)
    qd_all[me] = qd_send[me]

    def turn(j):
        kt_win[j] = kv_win[j].T[:HD]

    def forward(t, c):
        i = source(t)

        @pl.when(t > 0)
        def _():
            kv_arrival(i).wait_recv()

        fw_copy(0, i).start()
        fw_copy(1, i).start()
        turn(n + i)
        return c

    lax.fori_loop(0, n, forward, 0)

    def send_qd(t, c):
        qd_copy(peer(t)).start()
        return c

    lax.fori_loop(1, n, send_qd, 0)

    def window(t, c):
        i = source(t)
        fw_copy(0, i).wait_recv()
        turn(i)
        fw_copy(1, i).wait_recv()
        turn(2 * n + i)
        return c

    lax.fori_loop(0, n, window, 0)

    lane = lax.broadcasted_iota(jnp.int32, (QB, 2 * HD), 1)

    def fold(x, op):
        return op(x.reshape(QB // 8, 8, QB), axis=0)

    def operands(i):
        qd = qd_all[i]
        zero = jnp.zeros_like(qd)
        qd2 = jnp.concatenate([jnp.where(lane < HD, qd, zero), jnp.where(lane < HD, zero, qd)], axis=0)
        return qd2, [meta[i * NNB + s] for s in range(NNB)]

    def scores(i, st, tops):
        qd2, ids = operands(i)
        top = None
        for s in range(NNB):
            r = lax.dot_general(
                kv_win[ids[s]], qd2, (((1,), (1,)), ((), ())), preferred_element_type=F32
            )
            st[s] = r
            m = fold(r[:, :QB], jnp.max)
            top = m if top is None else jnp.maximum(top, m)
        tops[...] = top

    def grads(i, st, tops, w):
        qd2, ids = operands(i)
        top = jnp.max(tops[...], axis=0, keepdims=True)
        total = jnp.zeros((8, QB), F32)
        delta = jnp.zeros((8, QB), F32)
        for s in range(NNB):
            e = jnp.exp(st[s, :, :QB] - top)
            total += fold(e, jnp.sum)
            delta += fold(e * st[s, :, QB:], jnp.sum)
            st[s, :, :QB] = e
        inv = 1.0 / jnp.sum(total, axis=0, keepdims=True)
        delta = jnp.sum(delta, axis=0, keepdims=True) * inv
        for s in range(NNB):
            p = st[s, :, :QB] * inv
            ds = p * (st[s, :, QB:] - delta)
            w[s * QB : (s + 1) * QB, :QB] = ds.astype(BF16)
            w[s * QB : (s + 1) * QB, QB:] = p.astype(BF16)
        dqt = jnp.zeros((HD, QB), F32)
        for s in range(0, NNB, 2):
            kt = jnp.concatenate([kt_win[ids[s]], kt_win[ids[s + 1]]], axis=1)
            dqt += jnp.dot(kt, w[s * QB : (s + 2) * QB, :QB], preferred_element_type=F32)
        dq_send[i] = (dqt * HD**-0.5).astype(BF16)
        for s in range(NNB):
            parts[i * NNB + s] = jnp.dot(
                w[s * QB : (s + 1) * QB, :], qd2, preferred_element_type=F32
            )

    scores(me, st0, tops0)

    def query(u, c):
        i0, i1, i2 = source(2 * u), source(2 * u + 1), source(lax.rem(2 * u + 2, n))
        qd_arrival(i1).wait_recv()

        @pl.when(2 * u + 2 < n)
        def _():
            qd_arrival(i2).wait_recv()

        scores(i1, st1, tops1)
        grads(i0, st0, tops0, w0)
        scores(i2, st0, tops0)
        grads(i1, st1, tops1, w1)

        @pl.when(u > 0)
        def _():
            dq_copy(i0).start()

        dq_copy(i1).start()
        return c

    lax.fori_loop(0, n // 2, query, 0)
    dq_recv[pl.ds(pl.multiple_of(me * HD, HD), HD)] = dq_send[me]

    def add(e, acc):
        x = parts[meta[at_order + e]]
        acc = x + jnp.where(meta[at_keep + e] > 0, acc, 0.0)
        run[e] = acc
        return acc

    lax.fori_loop(0, pairs, add, jnp.zeros((QB, 2 * HD), F32))

    def summed(j):
        return jnp.where(meta[at_has + j] > 0, run[meta[at_last + j]], 0.0)

    def share(t, c):
        i = peer(n - t)
        part_send[0, i] = summed(i).astype(BF16)
        pt_copy(0, i).start()
        part_send[1, i] = summed(2 * n + i).astype(BF16)
        pt_copy(1, i).start()
        return c

    lax.fori_loop(1, n + 1, share, 0)

    def gather_dq(t, c):
        dq_arrival(source(t)).wait_recv()
        return c


    def home(t, c):
        i = peer(n - t)
        pt_copy(0, i).wait_recv()
        pt_copy(1, i).wait_recv()
        x = summed(n + i) + part_recv[0, i].astype(F32) + part_recv[1, i].astype(F32)
        out_send[i] = x.astype(BF16)

        @pl.when(t < n)
        def _():
            ot_copy(i).start()

        @pl.when(t == n)
        def _():
            out_recv[me] = x.astype(BF16)

        return c

    lax.fori_loop(1, n + 1, home, 0)
    lax.fori_loop(1, n, gather_dq, 0)

    def gather_out(t, c):
        ot_arrival(source(t)).wait_recv()
        return c

    lax.fori_loop(1, n, gather_out, 0)

    def drain(t, c):
        to = peer(t)
        kv_copy(to).wait_send()
        qd_copy(to).wait_send()
        dq_copy(to).wait_send()
        ot_copy(to).wait_send()
        return c

    lax.fori_loop(1, n, drain, 0)

    def drain_sides(i, c):
        for side in (0, 1):
            fw_copy(side, i).wait_send()
            pt_copy(side, i).wait_send()
        return c

    lax.fori_loop(0, n, drain_sides, 0)


def unpack(n, dq_ref, out_ref, gq_ref, gk_ref, gv_ref):
    for p in range(n // 2):
        cols = slice(2 * HD * p, 2 * HD * (p + 1))
        gq_ref[:, cols] = dq_ref[cols].T
        a, b = out_ref[2 * p], out_ref[2 * p + 1]
        gk_ref[:, cols] = jnp.concatenate([a[:, :HD], b[:, :HD]], axis=1)
        gv_ref[:, cols] = jnp.concatenate([a[:, HD:], b[:, HD:]], axis=1)


def per_device(query_rows, key_rows, value_rows, out_grad, block_pairs):
    n = lax.axis_size("head")
    pairs = n * NNB
    place = lax.axis_index("blk")
    own = lax.dynamic_slice_in_dim(block_pairs, place * n, n, 0).reshape(pairs)
    ids = (own - (place - 1) * n) % (n * lax.axis_size("blk"))
    e = jnp.arange(pairs, dtype=jnp.int32)
    less = (ids[None, :] < ids[:, None]) | ((ids[None, :] == ids[:, None]) & (e[None, :] < e[:, None]))
    rank = jnp.sum(less.astype(jnp.int32), axis=1)
    at = rank[None, :] == e[:, None]
    order = jnp.sum(jnp.where(at, e[None, :], 0), axis=1)
    same = (ids[None, :] == ids[:, None]) & (e[None, :] < e[:, None])
    going_on = jnp.any(same, axis=1).astype(jnp.int32)
    keep = jnp.sum(jnp.where(at, going_on[None, :], 0), axis=1)
    j = jnp.arange(3 * n, dtype=jnp.int32)
    upto = jnp.sum((ids[None, :] <= j[:, None]).astype(jnp.int32), axis=1)
    has = jnp.any(ids[None, :] == j[:, None], axis=1).astype(jnp.int32)
    meta = jnp.concatenate([ids, order, keep, jnp.maximum(upto - 1, 0), has]).astype(jnp.int32)

    rows = jax.ShapeDtypeStruct((QB, n * HD), BF16)
    tile = (QB, 2 * HD)
    dma = pltpu.SemaphoreType.DMA
    vmem = pl.BlockSpec(memory_space=pltpu.VMEM)
    arrived = pl.pallas_call(
        functools.partial(kernel, n),
        out_shape=(
            jax.ShapeDtypeStruct((n * HD, QB), BF16),
            jax.ShapeDtypeStruct((n,) + tile, BF16),
        ),
        in_specs=[pl.BlockSpec(memory_space=pltpu.SMEM)] + [pl.BlockSpec(memory_space=pl.ANY)] * 4,
        out_specs=(vmem, vmem),
        scratch_shapes=[
            pltpu.VMEM((QB, n * HD), BF16),
            pltpu.VMEM((QB, n * HD), BF16),
            pltpu.VMEM((QB, n * HD), BF16),
            pltpu.VMEM((QB, n * HD), BF16),
            pltpu.VMEM((n,) + tile, BF16),
            pltpu.VMEM((n,) + tile, BF16),
            pltpu.VMEM((3 * n,) + tile, BF16),
            pltpu.VMEM((3 * n, HD, QB), BF16),
            pltpu.VMEM((n,) + tile, BF16),
            pltpu.VMEM((NNB, QB, 2 * QB), F32),
            pltpu.VMEM((NNB, QB, 2 * QB), F32),
            pltpu.VMEM((8, QB), F32),
            pltpu.VMEM((8, QB), F32),
            pltpu.VMEM((NNB * QB, 2 * QB), BF16),
            pltpu.VMEM((NNB * QB, 2 * QB), BF16),
            pltpu.VMEM((pairs,) + tile, F32),
            pltpu.VMEM((pairs,) + tile, F32),
            pltpu.VMEM((n, HD, QB), BF16),
            pltpu.VMEM((2, n) + tile, BF16),
            pltpu.VMEM((2, n) + tile, BF16),
            pltpu.VMEM((n,) + tile, BF16),
            dma((4,)),
            dma((n,)),
            dma((n,)),
            dma((2, n)),
            dma((2, n)),
            dma((n,)),
            dma((n,)),
            dma((n,)),
            dma((n,)),
            dma((2, n)),
            dma((2, n)),
            dma((n,)),
            dma((n,)),
        ],
        compiler_params=pltpu.CompilerParams(
            collective_id=0, has_side_effects=True, vmem_limit_bytes=60 * 1024 * 1024
        ),
    )(meta, query_rows, key_rows, value_rows, out_grad)
    return pl.pallas_call(
        functools.partial(unpack, n),
        out_shape=(rows, rows, rows),
        in_specs=[vmem, vmem],
        out_specs=(vmem, vmem, vmem),
    )(*arrived)


def solution(mesh):
    rows = P(("blk", "head"), None)
    return jax.shard_map(
        per_device,
        mesh=mesh,
        in_specs=(rows, rows, rows, rows, P()),
        out_specs=(rows, rows, rows),
        check_vma=False,
    )
```
